32 devices in a mesh: groups: 2 (over y), graph: 8 (over z, x), mp: 2 (over core).
Axes of the slice: x: 2, y: 2, z: 4, core: 2. Of those that a mesh axis runs over, the one named last changes fastest.
Arguments:
- edges: bfloat16 [16384, 512], P(('groups', 'graph'), 'mp'), parts along dimension 0, may hold values from -6 to 6
- basis: bfloat16 [64, 32768], P(None, ('groups', 'graph')), parts along dimension 1, may hold values from -6 to 6
- w_basis: bfloat16 [64, 512], P(None, 'mp'), may hold values from -0.75 to 0.75
- w_up: bfloat16 [512, 512], P('mp'), may hold values from -0.25 to 0.25
- out_grad: bfloat16 [16384, 512], P(('groups', 'graph'), 'mp'), parts along dimension 0, may hold values from -6 to 6
- send_index: int32 [16, 256], P(('groups', 'graph')), parts along dimension 0, may hold values from 0 to 1023
- trip_slot: int32 [32768], P(('groups', 'graph')), parts along dimension 0, may hold values from 0 to 1279, as said below
- trip_out: int32 [32768], P(('groups', 'graph')), parts along dimension 0, may hold values from 0 to 1023
Outputs:
- grad_edges: bfloat16 [16384, 512], P(('groups', 'graph'), 'mp'), parts along dimension 0
- grad_w_up: float32 [1024, 512], P(('groups', 'mp')), parts along dimension 0
- grad_w_basis: float32 [128, 512], P('groups', 'mp'), parts along dimension 0
The draws below stay inside these ranges and needn't reach their ends.
There are 2 independent parts, one for each index of `groups`. The reference program is written for one: setup_inputs(seed, part) draws one part's arguments, and reference() takes and returns one part's arrays. A program takes and returns all parts, laid end to end along the dimension named above; an argument that names none is the same for every part. Nothing has to cross between parts.
Inputs may be any that keep to these rules, and one draw needn't show every extreme that they name: `trip_slot`: A value v below 1024 is a local edge of the triplet's shard; a value v of 1024 or more names row (v - 1024) % 32 of the rows that graph shard (v - 1024) // 32 packs for this shard by send_index, and only live rows are named. Each shard has between 8 and 32 live rows for each peer; every shard has all 32 live for graph shard 0 and for the next shard.
All inputs are finite; a program needn't handle non-finite values.
Results may differ from the reference program's by a relative error of at most 0.0059.
Values may be sent and summed in bfloat16 or wider, within the bound.
No kernel may reach another device: no remote copies, remote signals or barrier semaphores. Data moves between devices by JAX's collectives and lax.ppermute only.
A program may use at most 64 MiB of HBM per device.

```python
import jax
import jax.numpy as jnp
from jax import lax

DE = 512
BASIS = 64
E_DEV = 1024
CAP = 32
TRIP_DEV = 2048
EDGES = 8192
TRIPLETS = 16384
N_GRAPH = 8


def live_counts(key):
    lowest = jax.random.randint(key, (N_GRAPH, N_GRAPH), CAP // 4, CAP + 1)
    senders = jnp.arange(N_GRAPH)[:, None]
    targets = jnp.arange(N_GRAPH)[None, :]
    filled = (targets == 0) | (targets == (senders + 1) % N_GRAPH)
    return jnp.where(filled, CAP, lowest).astype(jnp.int32)


def draw_trip_slot(key, part):
    counts = live_counts(key)
    key = jax.random.fold_in(key, 7)
    key_local, key_source, key_row, key_pick = jax.random.split(key, 4)
    shard = (jnp.arange(TRIPLETS) // TRIP_DEV).astype(jnp.int32)
    local = jax.random.randint(key_local, (TRIPLETS,), 0, E_DEV)
    source = jax.random.randint(key_source, (TRIPLETS,), 0, N_GRAPH)
    raw = jax.random.randint(key_row, (TRIPLETS,), 0, 1 << 20)
    row = raw % counts[source, shard]
    remote = E_DEV + source * CAP + row
    pick = jax.random.randint(key_pick, (TRIPLETS,), 0, 2)
    result = jnp.where(pick == 1, remote, local)
    result = result.at[0].set(E_DEV + N_GRAPH * CAP - 1).at[1].set(0)
    return result.astype(jnp.int32)


def plant(values, key, low, top_value):
    place = [jax.random.randint(jax.random.fold_in(key, axis), (), 0, length) for axis, length in enumerate(values.shape)]
    longest = values.shape.index(max(values.shape))
    neighbour = place[:longest] + [(place[longest] + 1) % values.shape[longest]] + place[longest + 1:]
    return values.at[tuple(place)].set(low).at[tuple(neighbour)].set(top_value)


def levels(rng, extent, cuts, low, high):
    def one(axis_at, shards_of):
        heights = jax.random.uniform(jax.random.fold_in(jax.random.fold_in(rng, 6), axis_at), (shards_of,), jnp.float32, low / len(cuts), high / len(cuts))
        return jnp.repeat(jnp.exp(heights), extent[axis_at] // shards_of).reshape((-1,) + (1,) * (len(extent) - axis_at - 1))

    loudness = one(*cuts[0])
    for cut in cuts[1:]:
        loudness = loudness * one(*cut)
    return loudness


def noise(own_key, shape, deviation, limit, cuts=(), held_as=jnp.bfloat16):
    array = jax.random.normal(own_key, shape, jnp.float32) * deviation
    if len(cuts) > 0:
        array = levels(own_key, shape, cuts, -0.22, 0.18) * array
    return jnp.clip(array, min=-limit, max=limit).astype(held_as)


def setup_inputs(seed: int = 0, part: int = 0) -> dict:
    key_of = jax.random.split(jax.random.key(seed), 9)
    own_keys = jax.random.split(jax.random.fold_in(key_of[8], part), 9)
    edges = noise(own_keys[0], (EDGES, DE), 1.0, 6.0, ((0, 8), (1, 2)))
    basis = noise(own_keys[1], (BASIS, TRIPLETS), 1.0, 6.0, ((1, 8),))
    w_basis = noise(key_of[2], (BASIS, DE), BASIS ** -0.5, 0.75, ((1, 2),))
    w_up = noise(key_of[3], (DE, DE), DE ** -0.5, 0.25, ((0, 2),))
    out_grad = noise(own_keys[4], (EDGES, DE), 1.0, 6.0, ((0, 8), (1, 2)))
    send_index = plant(jax.random.randint(own_keys[5], (N_GRAPH, N_GRAPH * CAP), 0, E_DEV), jax.random.fold_in(own_keys[5], 1), 0, E_DEV - 1).astype(jnp.int32)
    trip_slot = draw_trip_slot(jax.random.fold_in(jax.random.fold_in(key_of[8], part), 71), part)
    trip_out = plant(jax.random.randint(own_keys[7], (TRIPLETS,), 0, E_DEV), jax.random.fold_in(own_keys[7], 1), 0, E_DEV - 1).astype(jnp.int32)
    return dict(edges=edges, basis=basis, w_basis=w_basis, w_up=w_up, out_grad=out_grad, send_index=send_index, trip_slot=trip_slot, trip_out=trip_out)


def project(bas, w_basis):
    return lax.dot_general(bas, w_basis, (((0,), (0,)), ((), ())), preferred_element_type=jnp.float32)


def reference(edges, basis, w_basis, w_up, out_grad, send_index, trip_slot, trip_out):
    width = edges.shape[1]
    shard = (jnp.arange(TRIPLETS) // TRIP_DEV).astype(jnp.int32)
    remote = jnp.maximum(trip_slot - E_DEV, 0).astype(jnp.int32)
    source = (remote // CAP).astype(jnp.int32)
    sent = send_index[source, shard * CAP + remote % CAP]
    in_edge = jnp.where(trip_slot < E_DEV, shard * E_DEV + trip_slot, source * E_DEV + sent).astype(jnp.int32)
    in_blocks = in_edge.reshape(N_GRAPH, TRIP_DEV)
    out_blocks = trip_out.reshape(N_GRAPH, TRIP_DEV)
    basis_blocks = basis.reshape(BASIS, N_GRAPH, TRIP_DEV).transpose(1, 0, 2)

    def agg_block(args):
        in_b, out_b, bas = args
        proj = project(bas, w_basis)
        rows = edges[in_b].astype(jnp.float32)
        return jax.ops.segment_sum(rows * proj, out_b, num_segments=E_DEV)

    agg = lax.map(agg_block, (in_blocks, out_blocks, basis_blocks)).reshape(EDGES, width).astype(jnp.bfloat16)
    pre = jnp.dot(agg, w_up, preferred_element_type=jnp.float32)
    sig = jax.nn.sigmoid(pre)
    g_pre = (out_grad.astype(jnp.float32) * sig * (1.0 + pre * (1.0 - sig))).astype(jnp.bfloat16)
    grad_w_up = lax.dot_general(agg, g_pre, (((0,), (0,)), ((), ())), preferred_element_type=jnp.float32) * (EDGES ** -0.5)
    g_agg = lax.dot_general(g_pre, w_up, (((1,), (1,)), ((), ())), preferred_element_type=jnp.float32)

    def back(carry, args):
        grad_rows, grad_bas = carry
        in_b, out_b, bas, index = args
        proj = project(bas, w_basis)
        local_grad = lax.dynamic_slice_in_dim(g_agg, (index * E_DEV).astype(jnp.int32), E_DEV, 0)
        g_y = local_grad[out_b]
        rows = edges[in_b].astype(jnp.float32)
        tgrad = (g_y * rows).astype(jnp.bfloat16)
        grad_bas = grad_bas + jnp.dot(bas, tgrad, preferred_element_type=jnp.float32)
        grad_rows = grad_rows.at[in_b].add(g_y * proj)
        return (grad_rows, grad_bas), None

    start = (jnp.zeros((EDGES, width), jnp.float32), jnp.zeros((BASIS, width), jnp.float32))
    indices = jnp.arange(N_GRAPH).astype(jnp.int32)
    (grad_rows, grad_bas), unused = lax.scan(back, start, (in_blocks, out_blocks, basis_blocks, indices))
    return grad_rows.astype(jnp.bfloat16), grad_w_up, grad_bas * (TRIPLETS ** -0.5)
```

```python
import functools

import jax
import jax.numpy as jnp
from jax import lax
from jax.experimental import pallas as pl
from jax.experimental.pallas import tpu as pltpu
from jax.sharding import PartitionSpec as P

BF16 = jnp.bfloat16
F32 = jnp.float32
LANES = 128
BLOCK = 512
VMEM_LIMIT = 16 * 1024 * 1024


def as_column(row):
    return jnp.broadcast_to(row, (LANES, LANES)).T


def select_rows(index_ref, first, length, count, base):
    wide = lax.broadcasted_iota(jnp.int32, (LANES, count), 1) + base
    parts = []
    for at in range(first // LANES, (first + length) // LANES):
        column = as_column(index_ref[at : at + 1, :])
        parts.append(jnp.where(jnp.tile(column, (1, count // LANES)) == wide, 1.0, 0.0).astype(BF16))
    return jnp.concatenate(parts, axis=0)


def select_columns(index_ref, first, length, count, base):
    tall = lax.broadcasted_iota(jnp.int32, (count, LANES), 0) + base
    parts = []
    for at in range(first // LANES, (first + length) // LANES):
        parts.append(jnp.where(index_ref[at : at + 1, :] == tall, 1.0, 0.0).astype(BF16))
    return jnp.concatenate(parts, axis=1)


def dot(a, b):
    return jnp.dot(a, b, preferred_element_type=F32)


def dot_tn(a, b):
    return lax.dot_general(a, b, (((0,), (0,)), ((), ())), preferred_element_type=F32)


def dot_nt(a, b):
    return lax.dot_general(a, b, (((1,), (1,)), ((), ())), preferred_element_type=F32)


def pack_kernel(send_ref, edges_ref, out_ref):
    rows = out_ref.shape[0]
    step = min(rows, BLOCK)
    for at in range(0, rows, step):
        select = select_rows(send_ref, at, step, edges_ref.shape[0], 0)
        out_ref[at : at + step, :] = dot(select, edges_ref[...]).astype(BF16)


def near_kernel(slot_ref, edges_ref, out_ref):
    for at in range(0, out_ref.shape[0], BLOCK):
        select = select_rows(slot_ref, at, BLOCK, edges_ref.shape[0], 0)
        out_ref[at : at + BLOCK, :] = dot(select, edges_ref[...]).astype(BF16)


def agg_kernel(slot_ref, out_index_ref, recv_ref, near_ref, basis_ref, wb_ref, rows_ref, agg_ref, msg_ref):
    trips, width = near_ref.shape
    edge_rows = agg_ref.shape[0]
    for at in range(0, trips, BLOCK):
        select = select_rows(slot_ref, at, BLOCK, recv_ref.shape[0], edge_rows)
        row = near_ref[at : at + BLOCK, :].astype(F32) + dot(select, recv_ref[...])
        rows_ref[at : at + BLOCK, :] = row.astype(BF16)
        message = row * dot_tn(basis_ref[:, at : at + BLOCK], wb_ref[...])
        top = message.astype(BF16)
        msg_ref[at : at + BLOCK, :width] = top
        msg_ref[at : at + BLOCK, width:] = (message - top.astype(F32)).astype(BF16)
    half = edge_rows // 2
    for top in range(0, edge_rows, half):
        select = select_columns(out_index_ref, 0, trips, half, top)
        both = dot(select, msg_ref[...])
        agg_ref[top : top + half, :] = (both[:, :width] + both[:, width:]).astype(BF16)


def slope_kernel(where_ref, own_ref, other_ref, w_own_ref, w_other_ref, cot_own_ref, cot_other_ref,
                 keep_ref, send_ref, g_ref):
    rows, half = own_ref.shape
    side = where_ref[0]
    bit = where_ref[1]
    quarter = half // 2
    for which, cot_ref in ((0, cot_own_ref), (1, cot_other_ref)):
        here = pl.multiple_of((side if which == 0 else 1 - side) * half, half)
        columns = pl.ds(here, half)
        pre = dot(own_ref[...], w_own_ref[:, columns]) + dot(other_ref[...], w_other_ref[:, columns])
        sig = 0.5 * jnp.tanh(0.5 * pre) + 0.5
        g = cot_ref[...].astype(F32) * sig * (1.0 + pre * (1.0 - sig))
        g_ref[:, columns] = g.astype(BF16)
    g = g_ref[...]
    kept = own_ref[:, pl.ds(pl.multiple_of(bit * quarter, quarter), quarter)]
    sent = own_ref[:, pl.ds(pl.multiple_of((1 - bit) * quarter, quarter), quarter)]
    for cols, ref in ((sent, send_ref), (kept, keep_ref)):
        part = dot_tn(cols, g).astype(ref.dtype)
        ref[:quarter, :] = part[:, :half]
        ref[quarter:, :] = part[:, half:]


def spread_kernel(slot_ref, out_index_ref, g_ref, w_ref, rows_ref, basis_ref, wb_ref, flow_ref, ret_ref, gb_ref, g_agg_ref):
    trips = rows_ref.shape[0]
    edge_rows = g_ref.shape[0]
    g_agg_ref[...] = dot_nt(g_ref[...], w_ref[...]).astype(BF16)
    total = jnp.zeros(gb_ref.shape, F32)
    for at in range(0, trips, BLOCK):
        select = select_rows(out_index_ref, at, BLOCK, edge_rows, 0)
        g_y = dot(select, g_agg_ref[...])
        flow_ref[at : at + BLOCK, :] = (g_y * dot_tn(basis_ref[:, at : at + BLOCK], wb_ref[...])).astype(BF16)
        tgrad = (g_y * rows_ref[at : at + BLOCK, :].astype(F32)).astype(BF16)
        total = total + dot(basis_ref[:, at : at + BLOCK], tgrad)
    gb_ref[...] = total.astype(BF16)
    step = min(ret_ref.shape[0], 256)
    for top in range(0, ret_ref.shape[0], step):
        select = select_columns(slot_ref, 0, trips, step, edge_rows + top)
        ret_ref[top : top + step, :] = dot(select, flow_ref[...]).astype(BF16)


def finish_kernel(up_scale, basis_scale, where_ref, mine_ref, theirs_ref, up_ref, basis_ref):
    half = up_ref.shape[0]
    quarter = half // 2
    bit = where_ref[1]
    for spot, ref in ((bit, mine_ref), (1 - bit, theirs_ref)):
        rows = pl.ds(pl.multiple_of(spot * quarter, quarter), quarter)
        up_ref[rows, :half] = ref[:quarter, :].astype(F32) * up_scale
        up_ref[rows, half:] = ref[quarter:half, :].astype(F32) * up_scale
    basis_ref[...] = (mine_ref[half:, :].astype(F32) + theirs_ref[half:, :].astype(F32)) * basis_scale


def home_kernel(slot_ref, flow_ref, out_ref):
    rows = out_ref.shape[0]
    half = rows // 2
    for top in range(0, rows, half):
        select = select_columns(slot_ref, 0, flow_ref.shape[0], half, top)
        out_ref[top : top + half, :] = dot(select, flow_ref[...])


def back_kernel(send_ref, returned_ref, home_ref, out_ref):
    select = select_columns(send_ref, 0, returned_ref.shape[0], out_ref.shape[0], 0)
    out_ref[...] = (home_ref[...] + dot(select, returned_ref[...])).astype(BF16)


def call(kernel, outs, flops, *operands, scalars=0, scratch=(), name=None):
    whole = pl.BlockSpec(memory_space=pltpu.VMEM)
    scalar = pl.BlockSpec(memory_space=pltpu.SMEM)
    moved = sum(x.size * x.dtype.itemsize for x in operands) + sum(x.size * x.dtype.itemsize for x in outs)
    return pl.pallas_call(
        kernel,
        out_shape=outs,
        in_specs=[scalar if i < scalars else whole for i in range(len(operands))],
        out_specs=[whole] * len(outs),
        scratch_shapes=scratch,
        compiler_params=pltpu.CompilerParams(vmem_limit_bytes=VMEM_LIMIT),
        cost_estimate=pl.CostEstimate(flops=flops, bytes_accessed=moved, transcendentals=0),
        name=name,
    )(*operands)


def shape(rows, columns, dtype):
    return jax.ShapeDtypeStruct((rows, columns), dtype)


def bit_order(bits, core):
    return [(core + k) % bits for k in range(bits)]


def swap(values, n_graph, step):
    bits = n_graph.bit_length() - 1
    pairs = []
    for g in range(n_graph):
        for core in range(2):
            bit = bit_order(bits, core)[step]
            pairs.append((g * 2 + core, (g ^ (1 << bit)) * 2 + core))
    return lax.ppermute(values, ("graph", "mp"), pairs)


def plus(a, b):
    return a.astype(F32) + b.astype(F32)


def on_device(edges, basis, w_basis, w_up, out_grad, send_index, trip_slot, trip_out):
    n_graph = lax.axis_size("graph")
    bits = n_graph.bit_length() - 1
    edge_rows, half = edges.shape
    packed_rows = send_index.shape[1]
    capacity = packed_rows // n_graph
    trips = basis.shape[1]
    quarter = half // 2
    core = lax.axis_index("mp")
    first_bit = (lax.axis_index("graph") >> jnp.where(core == 0, 0, 1 % bits)) & 1
    place = jnp.stack([core, first_bit]).astype(jnp.int32)
    send = send_index.reshape(packed_rows // LANES, LANES)
    slots = trip_slot.reshape(trips // LANES, LANES)
    outs = trip_out.reshape(trips // LANES, LANES)

    (packed,) = call(pack_kernel, [shape(packed_rows, half, BF16)], 2 * packed_rows * edge_rows * half, send, edges, name="pack")
    received = lax.all_to_all(packed, "graph", 0, 0, tiled=True)
    w_other, cot_other = lax.ppermute((w_up, out_grad), "mp", [(0, 1), (1, 0)])
    (near,) = call(near_kernel, [shape(trips, half, BF16)], 0, slots, edges, name="near")
    rows, agg = call(
        agg_kernel,
        [shape(trips, half, BF16), shape(edge_rows, half, BF16)],
        2 * trips * (packed_rows + 2 * edge_rows) * half,
        slots, outs, received, near, basis, w_basis,
        scratch=[pltpu.VMEM((trips, 2 * half), BF16)],
        name="agg",
    )
    agg_other = lax.ppermute(agg, "mp", [(0, 1), (1, 0)])
    keep, sent, g = call(
        slope_kernel,
        [shape(half, half, F32), shape(half, half, BF16), shape(edge_rows, 2 * half, BF16)],
        12 * edge_rows * half * half,
        place, agg, agg_other, w_up, w_other, out_grad, cot_other,
        scalars=1,
        name="slope",
    )
    got = swap(sent, n_graph, 0)
    flow, leaving, gb = call(
        spread_kernel,
        [shape(trips, half, BF16), shape(packed_rows, half, BF16), shape(basis.shape[0], half, BF16)],
        2 * trips * (edge_rows + packed_rows) * half,
        slots, outs, g, w_up, rows, basis, w_basis,
        scratch=[pltpu.VMEM((edge_rows, half), BF16)],
        name="spread",
    )
    returned = lax.all_to_all(leaving, "graph", 0, 0, tiled=True)
    (home,) = call(home_kernel, [shape(edge_rows, half, F32)], 2 * trips * edge_rows * half, slots, flow, name="home")
    load = jnp.concatenate([plus(keep, got).astype(BF16), gb], axis=0)
    for step in range(1, bits):
        load = plus(load, swap(load, n_graph, step)).astype(BF16)
    last = swap(load, n_graph, 0)
    grad_w_up, grad_w_basis = call(
        functools.partial(finish_kernel, (edge_rows * n_graph) ** (-0.5), (trips * n_graph) ** (-0.5)),
        [shape(half, 2 * half, F32), shape(basis.shape[0], half, F32)],
        4 * half * half,
        place, load, last,
        scalars=1,
        name="finish",
    )
    (grad_edges,) = call(
        back_kernel, [shape(edge_rows, half, BF16)], 2 * packed_rows * edge_rows * half, send, returned, home, name="back"
    )
    return (grad_edges, grad_w_up, grad_w_basis)


def solution(mesh):
    placed = (
        P(("groups", "graph"), "mp"),
        P(None, ("groups", "graph")),
        P(None, "mp"),
        P("mp", None),
        P(("groups", "graph"), "mp"),
        P(("groups", "graph"), None),
        P(("groups", "graph")),
        P(("groups", "graph")),
    )
    return jax.shard_map(
        on_device,
        mesh=mesh,
        in_specs=placed,
        out_specs=(P(("groups", "graph"), "mp"), P(("groups", "mp"), None), P("groups", "mp")),
        check_vma=False,
    )
```

```python
import functools

import jax
import jax.numpy as jnp
from jax import lax
from jax.experimental import pallas as pl
from jax.experimental.pallas import tpu as pltpu
from jax.sharding import PartitionSpec as P

BF16 = jnp.bfloat16
F32 = jnp.float32
LANES = 128
BLOCK = 512
VMEM_LIMIT = 16 * 1024 * 1024


def as_column(row):
    return jnp.broadcast_to(row, (LANES, LANES)).T


def select_rows(index_ref, first, length, count, base):
    wide = lax.broadcasted_iota(jnp.int32, (LANES, count), 1) + base
    parts = []
    for at in range(first // LANES, (first + length) // LANES):
        column = as_column(index_ref[at : at + 1, :])
        parts.append(jnp.where(jnp.tile(column, (1, count // LANES)) == wide, 1.0, 0.0).astype(BF16))
    return jnp.concatenate(parts, axis=0)


def select_columns(index_ref, first, length, count, base):
    tall = lax.broadcasted_iota(jnp.int32, (count, LANES), 0) + base
    parts = []
    for at in range(first // LANES, (first + length) // LANES):
        parts.append(jnp.where(index_ref[at : at + 1, :] == tall, 1.0, 0.0).astype(BF16))
    return jnp.concatenate(parts, axis=1)


def dot(a, b):
    return jnp.dot(a, b, preferred_element_type=F32)


def dot_tn(a, b):
    return lax.dot_general(a, b, (((0,), (0,)), ((), ())), preferred_element_type=F32)


def dot_nt(a, b):
    return lax.dot_general(a, b, (((1,), (1,)), ((), ())), preferred_element_type=F32)


def pack(send_index, edges):
    rows = jnp.arange(edges.shape[0], dtype=jnp.int32)
    return dot((send_index[:, None] == rows[None, :]).astype(BF16), edges).astype(BF16)


def near_kernel(slot_ref, edges_ref, out_ref):
    for at in range(0, out_ref.shape[0], BLOCK):
        select = select_rows(slot_ref, at, BLOCK, edges_ref.shape[0], 0)
        out_ref[at : at + BLOCK, :] = dot(select, edges_ref[...]).astype(BF16)


def agg_kernel(slot_ref, out_index_ref, recv_ref, near_ref, basis_ref, wb_ref, rows_ref, agg_ref, msg_ref):
    trips, width = near_ref.shape
    edge_rows = agg_ref.shape[0]
    for at in range(0, trips, BLOCK):
        select = select_rows(slot_ref, at, BLOCK, recv_ref.shape[0], edge_rows)
        row = near_ref[at : at + BLOCK, :].astype(F32) + dot(select, recv_ref[...])
        rows_ref[at : at + BLOCK, :] = row.astype(BF16)
        message = row * dot_tn(basis_ref[:, at : at + BLOCK], wb_ref[...])
        top = message.astype(BF16)
        msg_ref[at : at + BLOCK, :width] = top
        msg_ref[at : at + BLOCK, width:] = (message - top.astype(F32)).astype(BF16)
    half = edge_rows // 2
    for top in range(0, edge_rows, half):
        select = select_columns(out_index_ref, 0, trips, half, top)
        both = dot(select, msg_ref[...])
        agg_ref[top : top + half, :] = (both[:, :width] + both[:, width:]).astype(BF16)


def ready_kernel(own_ref, w_ref, pre_ref, turned_ref):
    pre_ref[...] = dot(own_ref[...], w_ref[...])
    turned_ref[...] = own_ref[...].T


def slope_kernel(where_ref, pre_ref, turned_ref, other_ref, w_ref, cot_own_ref, cot_other_ref, keep_ref, send_ref, g_ref):
    half = other_ref.shape[1]
    quarter = half // 2
    side = where_ref[0]
    bit = where_ref[1]
    for spot, cot_ref in ((side, cot_own_ref), (1 - side, cot_other_ref)):
        columns = pl.ds(pl.multiple_of(spot * half, half), half)
        pre = pre_ref[:, columns] + dot(other_ref[...], w_ref[:, columns])
        sig = 0.5 * jnp.tanh(0.5 * pre) + 0.5
        g = cot_ref[...].astype(F32) * sig * (1.0 + pre * (1.0 - sig))
        g_ref[:, columns] = g.astype(BF16)
    for spot, ref in ((1 - bit, send_ref), (bit, keep_ref)):
        part = dot(turned_ref[pl.ds(pl.multiple_of(spot * quarter, quarter), quarter), :], g_ref[...]).astype(ref.dtype)
        ref[:quarter, :] = part[:, :half]
        ref[quarter:, :] = part[:, half:]


def spread_kernel(slot_ref, out_index_ref, g_ref, w_ref, rows_ref, basis_ref, wb_ref, flow_ref, ret_ref, gb_ref, g_agg_ref):
    trips = rows_ref.shape[0]
    edge_rows = g_ref.shape[0]
    g_agg_ref[...] = dot_nt(g_ref[...], w_ref[...]).astype(BF16)
    total = jnp.zeros(gb_ref.shape, F32)
    for at in range(0, trips, BLOCK):
        select = select_rows(out_index_ref, at, BLOCK, edge_rows, 0)
        g_y = dot(select, g_agg_ref[...])
        flow_ref[at : at + BLOCK, :] = (g_y * dot_tn(basis_ref[:, at : at + BLOCK], wb_ref[...])).astype(BF16)
        tgrad = (g_y * rows_ref[at : at + BLOCK, :].astype(F32)).astype(BF16)
        total = total + dot(basis_ref[:, at : at + BLOCK], tgrad)
    gb_ref[...] = total.astype(BF16)
    step = min(ret_ref.shape[0], 256)
    for top in range(0, ret_ref.shape[0], step):
        select = select_columns(slot_ref, 0, trips, step, edge_rows + top)
        ret_ref[top : top + step, :] = dot(select, flow_ref[...]).astype(BF16)


def home_kernel(slot_ref, flow_ref, out_ref):
    rows = out_ref.shape[0]
    half = rows // 2
    for top in range(0, rows, half):
        select = select_columns(slot_ref, 0, flow_ref.shape[0], half, top)
        out_ref[top : top + half, :] = dot(select, flow_ref[...])


def finish_kernel(up_scale, basis_scale, where_ref, send_ref, returned_ref, home_ref, mine_ref, theirs_ref,
                  edges_ref, up_ref, basis_ref):
    half = up_ref.shape[0]
    quarter = half // 2
    bit = where_ref[1]
    for spot, ref in ((bit, mine_ref), (1 - bit, theirs_ref)):
        rows = pl.ds(pl.multiple_of(spot * quarter, quarter), quarter)
        up_ref[rows, :half] = ref[:quarter, :].astype(F32) * up_scale
        up_ref[rows, half:] = ref[quarter:half, :].astype(F32) * up_scale
    basis_ref[...] = (mine_ref[half:, :].astype(F32) + theirs_ref[half:, :].astype(F32)) * basis_scale
    select = select_columns(send_ref, 0, returned_ref.shape[0], edges_ref.shape[0], 0)
    edges_ref[...] = (home_ref[...] + dot(select, returned_ref[...])).astype(BF16)


def call(kernel, outs, flops, *operands, scalars=0, scratch=(), name=None):
    whole = pl.BlockSpec(memory_space=pltpu.VMEM)
    scalar = pl.BlockSpec(memory_space=pltpu.SMEM)
    moved = sum(x.size * x.dtype.itemsize for x in operands) + sum(x.size * x.dtype.itemsize for x in outs)
    return pl.pallas_call(
        kernel,
        out_shape=outs,
        in_specs=[scalar if i < scalars else whole for i in range(len(operands))],
        out_specs=[whole] * len(outs),
        scratch_shapes=scratch,
        compiler_params=pltpu.CompilerParams(vmem_limit_bytes=VMEM_LIMIT),
        cost_estimate=pl.CostEstimate(flops=flops, bytes_accessed=moved, transcendentals=0),
        name=name,
    )(*operands)


def shape(rows, columns, dtype):
    return jax.ShapeDtypeStruct((rows, columns), dtype)


def bit_order(bits, core):
    return [(core + k) % bits for k in range(bits)]


def swap(values, n_graph, step):
    bits = n_graph.bit_length() - 1
    pairs = []
    for g in range(n_graph):
        for core in range(2):
            bit = bit_order(bits, core)[step]
            pairs.append((g * 2 + core, (g ^ (1 << bit)) * 2 + core))
    return lax.ppermute(values, ("graph", "mp"), pairs)


def plus(a, b):
    return a.astype(F32) + b.astype(F32)


def on_device(edges, basis, w_basis, w_up, out_grad, send_index, trip_slot, trip_out):
    n_graph = lax.axis_size("graph")
    bits = n_graph.bit_length() - 1
    edge_rows, half = edges.shape
    packed_rows = send_index.shape[1]
    capacity = packed_rows // n_graph
    trips = basis.shape[1]
    quarter = half // 2
    core = lax.axis_index("mp")
    first_bit = (lax.axis_index("graph") >> jnp.where(core == 0, 0, 1 % bits)) & 1
    place = jnp.stack([core, first_bit]).astype(jnp.int32)
    send = send_index.reshape(packed_rows // LANES, LANES)
    slots = trip_slot.reshape(trips // LANES, LANES)
    outs = trip_out.reshape(trips // LANES, LANES)

    received = lax.all_to_all(pack(send_index[0], edges), "graph", 0, 0, tiled=True)
    w_other, cot_other = lax.ppermute((w_up, out_grad), "mp", [(0, 1), (1, 0)])
    (near,) = call(near_kernel, [shape(trips, half, BF16)], 0, slots, edges, name="near")
    rows, agg = call(
        agg_kernel,
        [shape(trips, half, BF16), shape(edge_rows, half, BF16)],
        2 * trips * (packed_rows + 2 * edge_rows) * half,
        slots, outs, received, near, basis, w_basis,
        scratch=[pltpu.VMEM((trips, 2 * half), BF16)],
        name="agg",
    )
    agg_other = lax.ppermute(agg, "mp", [(0, 1), (1, 0)])
    pre_own, turned = call(
        ready_kernel,
        [shape(edge_rows, 2 * half, F32), shape(half, edge_rows, BF16)],
        4 * edge_rows * half * half,
        agg, w_up,
        name="ready",
    )
    keep, sent, g = call(
        slope_kernel,
        [shape(half, half, F32), shape(half, half, BF16), shape(edge_rows, 2 * half, BF16)],
        8 * edge_rows * half * half,
        place, pre_own, turned, agg_other, w_other, out_grad, cot_other,
        scalars=1,
        name="slope",
    )
    got = swap(sent, n_graph, 0)
    flow, leaving, gb = call(
        spread_kernel,
        [shape(trips, half, BF16), shape(packed_rows, half, BF16), shape(basis.shape[0], half, BF16)],
        2 * trips * (edge_rows + packed_rows) * half,
        slots, outs, g, w_up, rows, basis, w_basis,
        scratch=[pltpu.VMEM((edge_rows, half), BF16)],
        name="spread",
    )
    returned = lax.all_to_all(leaving, "graph", 0, 0, tiled=True)
    (home,) = call(home_kernel, [shape(edge_rows, half, F32)], 2 * trips * edge_rows * half, slots, flow, name="home")
    load = jnp.concatenate([plus(keep, got).astype(BF16), gb], axis=0)
    for step in range(1, bits):
        load = plus(load, swap(load, n_graph, step)).astype(BF16)
    last = swap(load, n_graph, 0)
    return call(
        functools.partial(finish_kernel, (edge_rows * n_graph) ** (-0.5), (trips * n_graph) ** (-0.5)),
        [shape(edge_rows, half, BF16), shape(half, 2 * half, F32), shape(basis.shape[0], half, F32)],
        2 * packed_rows * edge_rows * half,
        place, send, returned, home, load, last,
        scalars=1,
        name="finish",
    )


def solution(mesh):
    placed = (
        P(("groups", "graph"), "mp"),
        P(None, ("groups", "graph")),
        P(None, "mp"),
        P("mp", None),
        P(("groups", "graph"), "mp"),
        P(("groups", "graph"), None),
        P(("groups", "graph")),
        P(("groups", "graph")),
    )
    return jax.shard_map(
        on_device,
        mesh=mesh,
        in_specs=placed,
        out_specs=(P(("groups", "graph"), "mp"), P(("groups", "mp"), None), P("groups", "mp")),
        check_vma=False,
    )
```

```python
import functools

import jax
import jax.numpy as jnp
from jax import lax
from jax.experimental import pallas as pl
from jax.experimental.pallas import tpu as pltpu
from jax.sharding import PartitionSpec as P

BF16 = jnp.bfloat16
F32 = jnp.float32
LANES = 128
BLOCK = 512
VMEM_LIMIT = 16 * 1024 * 1024


def as_column(row):
    return jnp.broadcast_to(row, (LANES, LANES)).T


def select_rows(index_ref, first, length, count, base):
    wide = lax.broadcasted_iota(jnp.int32, (LANES, count), 1) + base
    parts = []
    for at in range(first // LANES, (first + length) // LANES):
        column = as_column(index_ref[at : at + 1, :])
        parts.append(jnp.where(jnp.tile(column, (1, count // LANES)) == wide, 1.0, 0.0).astype(BF16))
    return jnp.concatenate(parts, axis=0)


def select_columns(index_ref, first, length, count, base):
    tall = lax.broadcasted_iota(jnp.int32, (count, LANES), 0) + base
    parts = []
    for at in range(first // LANES, (first + length) // LANES):
        parts.append(jnp.where(index_ref[at : at + 1, :] == tall, 1.0, 0.0).astype(BF16))
    return jnp.concatenate(parts, axis=1)


def dot(a, b):
    return jnp.dot(a, b, preferred_element_type=F32)


def dot_tn(a, b):
    return lax.dot_general(a, b, (((0,), (0,)), ((), ())), preferred_element_type=F32)


def dot_nt(a, b):
    return lax.dot_general(a, b, (((1,), (1,)), ((), ())), preferred_element_type=F32)


def pack(send_index, edges):
    rows = jnp.arange(edges.shape[0], dtype=jnp.int32)
    return dot((send_index[:, None] == rows[None, :]).astype(BF16), edges).astype(BF16)


def near_kernel(where_ref, slot_ref, edges_ref, cot_own_hbm, cot_other_hbm, out_ref, cot_ref, sems):
    width = edges_ref.shape[1]
    side = where_ref[0]
    copies = []
    for k, (spot, hbm) in enumerate(((side, cot_own_hbm), (1 - side, cot_other_hbm))):
        columns = pl.ds(pl.multiple_of(spot * width, width), width)
        copies.append(pltpu.make_async_copy(hbm, cot_ref.at[:, columns], sems.at[k]))
        copies[-1].start()
    for at in range(0, out_ref.shape[0], BLOCK):
        select = select_rows(slot_ref, at, BLOCK, edges_ref.shape[0], 0)
        out_ref[at : at + BLOCK, :] = dot(select, edges_ref[...]).astype(BF16)
    for copy in copies:
        copy.wait()


def agg_kernel(slot_ref, out_index_ref, recv_ref, near_ref, basis_ref, wb_ref, rows_ref, agg_ref, msg_ref):
    trips, width = near_ref.shape
    edge_rows = agg_ref.shape[0]
    for at in range(0, trips, BLOCK):
        select = select_rows(slot_ref, at, BLOCK, recv_ref.shape[0], edge_rows)
        row = near_ref[at : at + BLOCK, :].astype(F32) + dot(select, recv_ref[...])
        rows_ref[at : at + BLOCK, :] = row.astype(BF16)
        message = row * dot_tn(basis_ref[:, at : at + BLOCK], wb_ref[...])
        top = message.astype(BF16)
        msg_ref[at : at + BLOCK, :width] = top
        msg_ref[at : at + BLOCK, width:] = (message - top.astype(F32)).astype(BF16)
    half = edge_rows // 2
    for top in range(0, edge_rows, half):
        select = select_columns(out_index_ref, 0, trips, half, top)
        both = dot(select, msg_ref[...])
        agg_ref[top : top + half, :] = (both[:, :width] + both[:, width:]).astype(BF16)


def ready_kernel(own_ref, w_ref, pre_ref, turned_ref):
    pre_ref[...] = dot(own_ref[...], w_ref[...])
    turned_ref[...] = own_ref[...].T


def slope_kernel(where_ref, pre_ref, turned_ref, other_ref, w_ref, cot_ref, keep_ref, send_ref, g_ref):
    half = other_ref.shape[1]
    quarter = half // 2
    bit = where_ref[1]
    for columns in (slice(0, half), slice(half, 2 * half)):
        pre = pre_ref[:, columns] + dot(other_ref[...], w_ref[:, columns])
        sig = 0.5 * jnp.tanh(0.5 * pre) + 0.5
        g = cot_ref[:, columns].astype(F32) * sig * (1.0 + pre * (1.0 - sig))
        g_ref[:, columns] = g.astype(BF16)
    for spot, ref in ((1 - bit, send_ref), (bit, keep_ref)):
        part = dot(turned_ref[pl.ds(pl.multiple_of(spot * quarter, quarter), quarter), :], g_ref[...]).astype(ref.dtype)
        ref[:quarter, :] = part[:, :half]
        ref[quarter:, :] = part[:, half:]


def spread_kernel(slot_ref, out_index_ref, g_ref, w_ref, rows_ref, basis_ref, wb_ref, flow_ref, ret_ref, gb_ref, g_agg_ref):
    trips = rows_ref.shape[0]
    edge_rows = g_ref.shape[0]
    g_agg_ref[...] = dot_nt(g_ref[...], w_ref[...]).astype(BF16)
    total = jnp.zeros(gb_ref.shape, F32)
    for at in range(0, trips, BLOCK):
        select = select_rows(out_index_ref, at, BLOCK, edge_rows, 0)
        g_y = dot(select, g_agg_ref[...])
        flow_ref[at : at + BLOCK, :] = (g_y * dot_tn(basis_ref[:, at : at + BLOCK], wb_ref[...])).astype(BF16)
        tgrad = (g_y * rows_ref[at : at + BLOCK, :].astype(F32)).astype(BF16)
        total = total + dot(basis_ref[:, at : at + BLOCK], tgrad)
    gb_ref[...] = total.astype(BF16)
    step = min(ret_ref.shape[0], 256)
    for top in range(0, ret_ref.shape[0], step):
        select = select_columns(slot_ref, 0, trips, step, edge_rows + top)
        ret_ref[top : top + step, :] = dot(select, flow_ref[...]).astype(BF16)


def home_kernel(slot_ref, flow_ref, out_ref):
    rows = out_ref.shape[0]
    half = rows // 2
    for top in range(0, rows, half):
        select = select_columns(slot_ref, 0, flow_ref.shape[0], half, top)
        out_ref[top : top + half, :] = dot(select, flow_ref[...])


def finish_kernel(up_scale, basis_scale, where_ref, send_ref, returned_ref, home_ref, mine_ref, theirs_ref,
                  edges_ref, up_ref, basis_ref):
    half = up_ref.shape[0]
    quarter = half // 2
    bit = where_ref[1]
    for spot, ref in ((bit, mine_ref), (1 - bit, theirs_ref)):
        rows = pl.ds(pl.multiple_of(spot * quarter, quarter), quarter)
        up_ref[rows, :half] = ref[:quarter, :].astype(F32) * up_scale
        up_ref[rows, half:] = ref[quarter:half, :].astype(F32) * up_scale
    basis_ref[...] = (mine_ref[half:, :].astype(F32) + theirs_ref[half:, :].astype(F32)) * basis_scale
    select = select_columns(send_ref, 0, returned_ref.shape[0], edges_ref.shape[0], 0)
    edges_ref[...] = (home_ref[...] + dot(select, returned_ref[...])).astype(BF16)


def call(kernel, outs, flops, *operands, scalars=0, far=0, scratch=(), name=None):
    whole = pl.BlockSpec(memory_space=pltpu.VMEM)
    scalar = pl.BlockSpec(memory_space=pltpu.SMEM)
    place = pl.BlockSpec(memory_space=pl.ANY)
    near = len(operands) - far
    moved = sum(x.size * x.dtype.itemsize for x in operands) + sum(x.size * x.dtype.itemsize for x in outs)
    return pl.pallas_call(
        kernel,
        out_shape=outs,
        in_specs=[scalar if i < scalars else whole if i < near else place for i in range(len(operands))],
        out_specs=[whole] * len(outs),
        scratch_shapes=scratch,
        compiler_params=pltpu.CompilerParams(vmem_limit_bytes=VMEM_LIMIT),
        cost_estimate=pl.CostEstimate(flops=flops, bytes_accessed=moved, transcendentals=0),
        name=name,
    )(*operands)


def shape(rows, columns, dtype):
    return jax.ShapeDtypeStruct((rows, columns), dtype)


def bit_order(bits, core):
    return [(core + k) % bits for k in range(bits)]


def swap(values, n_graph, step):
    bits = n_graph.bit_length() - 1
    pairs = []
    for g in range(n_graph):
        for core in range(2):
            bit = bit_order(bits, core)[step]
            pairs.append((g * 2 + core, (g ^ (1 << bit)) * 2 + core))
    return lax.ppermute(values, ("graph", "mp"), pairs)


def plus(a, b):
    return a.astype(F32) + b.astype(F32)


def on_device(edges, basis, w_basis, w_up, out_grad, send_index, trip_slot, trip_out):
    n_graph = lax.axis_size("graph")
    bits = n_graph.bit_length() - 1
    edge_rows, half = edges.shape
    packed_rows = send_index.shape[1]
    capacity = packed_rows // n_graph
    trips = basis.shape[1]
    quarter = half // 2
    core = lax.axis_index("mp")
    first_bit = (lax.axis_index("graph") >> jnp.where(core == 0, 0, 1 % bits)) & 1
    place = jnp.stack([core, first_bit]).astype(jnp.int32)
    send = send_index.reshape(packed_rows // LANES, LANES)
    slots = trip_slot.reshape(trips // LANES, LANES)
    outs = trip_out.reshape(trips // LANES, LANES)

    received = lax.all_to_all(pack(send_index[0], edges), "graph", 0, 0, tiled=True)
    w_other, cot_other = lax.ppermute((w_up, out_grad), "mp", [(0, 1), (1, 0)])
    near, cot = call(
        near_kernel,
        [shape(trips, half, BF16), shape(edge_rows, 2 * half, BF16)],
        0,
        place, slots, edges, out_grad, cot_other,
        scalars=1,
        far=2,
        scratch=[pltpu.SemaphoreType.DMA((2,))],
        name="near",
    )
    rows, agg = call(
        agg_kernel,
        [shape(trips, half, BF16), shape(edge_rows, half, BF16)],
        2 * trips * (packed_rows + 2 * edge_rows) * half,
        slots, outs, received, near, basis, w_basis,
        scratch=[pltpu.VMEM((trips, 2 * half), BF16)],
        name="agg",
    )
    agg_other = lax.ppermute(agg, "mp", [(0, 1), (1, 0)])
    pre_own, turned = call(
        ready_kernel,
        [shape(edge_rows, 2 * half, F32), shape(half, edge_rows, BF16)],
        4 * edge_rows * half * half,
        agg, w_up,
        name="ready",
    )
    keep, sent, g = call(
        slope_kernel,
        [shape(half, half, F32), shape(half, half, BF16), shape(edge_rows, 2 * half, BF16)],
        8 * edge_rows * half * half,
        place, pre_own, turned, agg_other, w_other, cot,
        scalars=1,
        name="slope",
    )
    got = swap(sent, n_graph, 0)
    flow, leaving, gb = call(
        spread_kernel,
        [shape(trips, half, BF16), shape(packed_rows, half, BF16), shape(basis.shape[0], half, BF16)],
        2 * trips * (edge_rows + packed_rows) * half,
        slots, outs, g, w_up, rows, basis, w_basis,
        scratch=[pltpu.VMEM((edge_rows, half), BF16)],
        name="spread",
    )
    returned = lax.all_to_all(leaving, "graph", 0, 0, tiled=True)
    (home,) = call(home_kernel, [shape(edge_rows, half, F32)], 2 * trips * edge_rows * half, slots, flow, name="home")
    load = jnp.concatenate([plus(keep, got).astype(BF16), gb], axis=0)
    for step in range(1, bits):
        load = plus(load, swap(load, n_graph, step)).astype(BF16)
    last = swap(load, n_graph, 0)
    return call(
        functools.partial(finish_kernel, (edge_rows * n_graph) ** (-0.5), (trips * n_graph) ** (-0.5)),
        [shape(edge_rows, half, BF16), shape(half, 2 * half, F32), shape(basis.shape[0], half, F32)],
        2 * packed_rows * edge_rows * half,
        place, send, returned, home, load, last,
        scalars=1,
        name="finish",
    )


def solution(mesh):
    placed = (
        P(("groups", "graph"), "mp"),
        P(None, ("groups", "graph")),
        P(None, "mp"),
        P("mp", None),
        P(("groups", "graph"), "mp"),
        P(("groups", "graph"), None),
        P(("groups", "graph")),
        P(("groups", "graph")),
    )
    return jax.shard_map(
        on_device,
        mesh=mesh,
        in_specs=placed,
        out_specs=(P(("groups", "graph"), "mp"), P(("groups", "mp"), None), P("groups", "mp")),
        check_vma=False,
    )
```

```python
import functools

import jax
import jax.numpy as jnp
from jax import lax
from jax.experimental import pallas as pl
from jax.experimental.pallas import tpu as pltpu
from jax.sharding import PartitionSpec as P

BF16 = jnp.bfloat16
F32 = jnp.float32
LANES = 128
BLOCK = 512
VMEM_LIMIT = 16 * 1024 * 1024


def as_column(row):
    return jnp.broadcast_to(row, (LANES, LANES)).T


def select_rows(index_ref, first, length, count, base):
    wide = lax.broadcasted_iota(jnp.int32, (LANES, count), 1) + base
    parts = []
    for at in range(first // LANES, (first + length) // LANES):
        column = as_column(index_ref[at : at + 1, :])
        parts.append(jnp.where(jnp.tile(column, (1, count // LANES)) == wide, 1.0, 0.0).astype(BF16))
    return jnp.concatenate(parts, axis=0)


def select_columns(index_ref, first, length, count, base):
    tall = lax.broadcasted_iota(jnp.int32, (count, LANES), 0) + base
    parts = []
    for at in range(first // LANES, (first + length) // LANES):
        parts.append(jnp.where(index_ref[at : at + 1, :] == tall, 1.0, 0.0).astype(BF16))
    return jnp.concatenate(parts, axis=1)


def dot(a, b):
    return jnp.dot(a, b, preferred_element_type=F32)


def dot_tn(a, b):
    return lax.dot_general(a, b, (((0,), (0,)), ((), ())), preferred_element_type=F32)


def dot_nt(a, b):
    return lax.dot_general(a, b, (((1,), (1,)), ((), ())), preferred_element_type=F32)


def pack(send_index, edges):
    rows = jnp.arange(edges.shape[0], dtype=jnp.int32)
    return jnp.dot((send_index[:, None] == rows[None, :]).astype(BF16), edges, preferred_element_type=BF16)


def near_kernel(where_ref, slot_ref, edges_ref, cot_own_hbm, cot_other_hbm, out_ref, cot_ref, sems):
    width = edges_ref.shape[1]
    side = where_ref[0]
    copies = []
    for k, (spot, hbm) in enumerate(((side, cot_own_hbm), (1 - side, cot_other_hbm))):
        columns = pl.ds(pl.multiple_of(spot * width, width), width)
        copies.append(pltpu.make_async_copy(hbm, cot_ref.at[:, columns], sems.at[k]))
        copies[-1].start()
    for at in range(0, out_ref.shape[0], BLOCK):
        select = select_rows(slot_ref, at, BLOCK, edges_ref.shape[0], 0)
        out_ref[at : at + BLOCK, :] = dot(select, edges_ref[...]).astype(BF16)
    for copy in copies:
        copy.wait()


def agg_kernel(slot_ref, out_index_ref, recv_ref, near_ref, basis_ref, wb_ref, rows_ref, agg_ref, msg_ref):
    trips, width = near_ref.shape
    edge_rows = agg_ref.shape[0]
    for at in range(0, trips, BLOCK):
        select = select_rows(slot_ref, at, BLOCK, recv_ref.shape[0], edge_rows)
        row = near_ref[at : at + BLOCK, :].astype(F32) + dot(select, recv_ref[...])
        rows_ref[at : at + BLOCK, :] = row.astype(BF16)
        message = row * dot_tn(basis_ref[:, at : at + BLOCK], wb_ref[...])
        top = message.astype(BF16)
        msg_ref[at : at + BLOCK, :width] = top
        msg_ref[at : at + BLOCK, width:] = (message - top.astype(F32)).astype(BF16)
    half = edge_rows // 2
    for top in range(0, edge_rows, half):
        select = select_columns(out_index_ref, 0, trips, half, top)
        both = dot(select, msg_ref[...])
        agg_ref[top : top + half, :] = (both[:, :width] + both[:, width:]).astype(BF16)


def ready_kernel(own_ref, w_ref, pre_ref, turned_ref):
    pre_ref[...] = dot(own_ref[...], w_ref[...])
    turned_ref[...] = own_ref[...].T


def slope_kernel(where_ref, pre_ref, turned_ref, other_ref, w_ref, cot_ref, keep_ref, send_ref, g_ref):
    half = other_ref.shape[1]
    quarter = half // 2
    bit = where_ref[1]
    for columns in (slice(0, half), slice(half, 2 * half)):
        pre = pre_ref[:, columns] + dot(other_ref[...], w_ref[:, columns])
        sig = 0.5 * jnp.tanh(0.5 * pre) + 0.5
        g = cot_ref[:, columns].astype(F32) * sig * (1.0 + pre * (1.0 - sig))
        g_ref[:, columns] = g.astype(BF16)
    for spot, ref in ((1 - bit, send_ref), (bit, keep_ref)):
        part = dot(turned_ref[pl.ds(pl.multiple_of(spot * quarter, quarter), quarter), :], g_ref[...]).astype(ref.dtype)
        ref[:quarter, :] = part[:, :half]
        ref[quarter:, :] = part[:, half:]


def spread_kernel(slot_ref, out_index_ref, g_ref, w_ref, rows_ref, basis_ref, wb_ref, flow_ref, ret_ref, gb_ref, g_agg_ref):
    trips = rows_ref.shape[0]
    edge_rows = g_ref.shape[0]
    g_agg_ref[...] = dot_nt(g_ref[...], w_ref[...]).astype(BF16)
    total = jnp.zeros(gb_ref.shape, F32)
    for at in range(0, trips, BLOCK):
        select = select_rows(out_index_ref, at, BLOCK, edge_rows, 0)
        g_y = dot(select, g_agg_ref[...])
        flow_ref[at : at + BLOCK, :] = (g_y * dot_tn(basis_ref[:, at : at + BLOCK], wb_ref[...])).astype(BF16)
        tgrad = (g_y * rows_ref[at : at + BLOCK, :].astype(F32)).astype(BF16)
        total = total + dot(basis_ref[:, at : at + BLOCK], tgrad)
    gb_ref[...] = total.astype(BF16)
    step = min(ret_ref.shape[0], 256)
    for top in range(0, ret_ref.shape[0], step):
        select = select_columns(slot_ref, 0, trips, step, edge_rows + top)
        ret_ref[top : top + step, :] = dot(select, flow_ref[...]).astype(BF16)


def home_kernel(slot_ref, flow_ref, out_ref):
    rows = out_ref.shape[0]
    half = rows // 2
    for top in range(0, rows, half):
        select = select_columns(slot_ref, 0, flow_ref.shape[0], half, top)
        out_ref[top : top + half, :] = dot(select, flow_ref[...])


def finish_kernel(up_scale, basis_scale, where_ref, send_ref, returned_ref, home_ref, mine_ref, theirs_ref,
                  edges_ref, up_ref, basis_ref):
    half = up_ref.shape[0]
    quarter = half // 2
    bit = where_ref[1]
    for spot, ref in ((bit, mine_ref), (1 - bit, theirs_ref)):
        rows = pl.ds(pl.multiple_of(spot * quarter, quarter), quarter)
        up_ref[rows, :half] = ref[:quarter, :].astype(F32) * up_scale
        up_ref[rows, half:] = ref[quarter:half, :].astype(F32) * up_scale
    basis_ref[...] = (mine_ref[half:, :].astype(F32) + theirs_ref[half:, :].astype(F32)) * basis_scale
    select = select_columns(send_ref, 0, returned_ref.shape[0], edges_ref.shape[0], 0)
    edges_ref[...] = (home_ref[...] + dot(select, returned_ref[...])).astype(BF16)


def call(kernel, outs, flops, *operands, scalars=0, far=0, scratch=(), name=None):
    whole = pl.BlockSpec(memory_space=pltpu.VMEM)
    scalar = pl.BlockSpec(memory_space=pltpu.SMEM)
    place = pl.BlockSpec(memory_space=pl.ANY)
    near = len(operands) - far
    moved = sum(x.size * x.dtype.itemsize for x in operands) + sum(x.size * x.dtype.itemsize for x in outs)
    return pl.pallas_call(
        kernel,
        out_shape=outs,
        in_specs=[scalar if i < scalars else whole if i < near else place for i in range(len(operands))],
        out_specs=[whole] * len(outs),
        scratch_shapes=scratch,
        compiler_params=pltpu.CompilerParams(vmem_limit_bytes=VMEM_LIMIT),
        cost_estimate=pl.CostEstimate(flops=flops, bytes_accessed=moved, transcendentals=0),
        name=name,
    )(*operands)


def shape(rows, columns, dtype):
    return jax.ShapeDtypeStruct((rows, columns), dtype)


def bit_order(bits, core):
    return [(core + k) % bits for k in range(bits)]


def swap(values, n_graph, step):
    bits = n_graph.bit_length() - 1
    pairs = []
    for g in range(n_graph):
        for core in range(2):
            bit = bit_order(bits, core)[step]
            pairs.append((g * 2 + core, (g ^ (1 << bit)) * 2 + core))
    return lax.ppermute(values, ("graph", "mp"), pairs)


def plus(a, b):
    return a.astype(F32) + b.astype(F32)


def on_device(edges, basis, w_basis, w_up, out_grad, send_index, trip_slot, trip_out):
    n_graph = lax.axis_size("graph")
    bits = n_graph.bit_length() - 1
    edge_rows, half = edges.shape
    packed_rows = send_index.shape[1]
    capacity = packed_rows // n_graph
    trips = basis.shape[1]
    quarter = half // 2
    core = lax.axis_index("mp")
    first_bit = (lax.axis_index("graph") >> jnp.where(core == 0, 0, 1 % bits)) & 1
    place = jnp.stack([core, first_bit]).astype(jnp.int32)
    send = send_index.reshape(packed_rows // LANES, LANES)
    slots = trip_slot.reshape(trips // LANES, LANES)
    outs = trip_out.reshape(trips // LANES, LANES)

    packed, cot_mine = lax.optimization_barrier((pack(send_index[0], edges), out_grad))
    received = lax.all_to_all(packed, "graph", 0, 0, tiled=True)
    w_other, cot_other = lax.ppermute((w_up, cot_mine), "mp", [(0, 1), (1, 0)])
    near, cot = call(
        near_kernel,
        [shape(trips, half, BF16), shape(edge_rows, 2 * half, BF16)],
        0,
        place, slots, edges, out_grad, cot_other,
        scalars=1,
        far=2,
        scratch=[pltpu.SemaphoreType.DMA((2,))],
        name="near",
    )
    rows, agg = call(
        agg_kernel,
        [shape(trips, half, BF16), shape(edge_rows, half, BF16)],
        2 * trips * (packed_rows + 2 * edge_rows) * half,
        slots, outs, received, near, basis, w_basis,
        scratch=[pltpu.VMEM((trips, 2 * half), BF16)],
        name="agg",
    )
    agg_other = lax.ppermute(agg, "mp", [(0, 1), (1, 0)])
    pre_own, turned = call(
        ready_kernel,
        [shape(edge_rows, 2 * half, F32), shape(half, edge_rows, BF16)],
        4 * edge_rows * half * half,
        agg, w_up,
        name="ready",
    )
    keep, sent, g = call(
        slope_kernel,
        [shape(half, half, F32), shape(half, half, BF16), shape(edge_rows, 2 * half, BF16)],
        8 * edge_rows * half * half,
        place, pre_own, turned, agg_other, w_other, cot,
        scalars=1,
        name="slope",
    )
    got = swap(sent, n_graph, 0)
    flow, leaving, gb = call(
        spread_kernel,
        [shape(trips, half, BF16), shape(packed_rows, half, BF16), shape(basis.shape[0], half, BF16)],
        2 * trips * (edge_rows + packed_rows) * half,
        slots, outs, g, w_up, rows, basis, w_basis,
        scratch=[pltpu.VMEM((edge_rows, half), BF16)],
        name="spread",
    )
    returned = lax.all_to_all(leaving, "graph", 0, 0, tiled=True)
    (home,) = call(home_kernel, [shape(edge_rows, half, F32)], 2 * trips * edge_rows * half, slots, flow, name="home")
    load = jnp.concatenate([plus(keep, got).astype(BF16), gb], axis=0)
    for step in range(1, bits):
        load = plus(load, swap(load, n_graph, step)).astype(BF16)
    last = swap(load, n_graph, 0)
    return call(
        functools.partial(finish_kernel, (edge_rows * n_graph) ** (-0.5), (trips * n_graph) ** (-0.5)),
        [shape(edge_rows, half, BF16), shape(half, 2 * half, F32), shape(basis.shape[0], half, F32)],
        2 * packed_rows * edge_rows * half,
        place, send, returned, home, load, last,
        scalars=1,
        name="finish",
    )


def solution(mesh):
    placed = (
        P(("groups", "graph"), "mp"),
        P(None, ("groups", "graph")),
        P(None, "mp"),
        P("mp", None),
        P(("groups", "graph"), "mp"),
        P(("groups", "graph"), None),
        P(("groups", "graph")),
        P(("groups", "graph")),
    )
    return jax.shard_map(
        on_device,
        mesh=mesh,
        in_specs=placed,
        out_specs=(P(("groups", "graph"), "mp"), P(("groups", "mp"), None), P("groups", "mp")),
        check_vma=False,
    )
```
